512 devices in a mesh: dp: 16 (over z), ep: 32 (over y, x, core).
Axes of the slice: x: 4, y: 4, z: 16, core: 2. Of those that a mesh axis runs over, the one named last changes fastest.
Arguments:
- upstream: bfloat16 [65536, 2880], P(('dp', 'ep')), may hold values from -6 to 6
- router_logits: float32 [65536, 4], P(('dp', 'ep')), may hold values from -4 to 4
- expert_ids: int32 [65536, 4], P(('dp', 'ep')), may hold values from 0 to 127, as said below
- guard_mask: int32 [65536], P(('dp', 'ep')), may hold values 0 or 1
- w_down: bfloat16 [11520, 2880], P('ep'), may hold values from -0.109375 to 0.109375
- saved_hidden: bfloat16 [11520, 16384], P('ep', 'dp'), may hold values from -0.59765625 to 0.59765625
Outputs:
- grad_hidden: bfloat16 [11520, 16384], P('ep', 'dp')
- grad_down: bfloat16 [2880, 11520], P('dp', 'ep')
- grad_logits: float32 [65536, 4], P(('dp', 'ep'))
The draws below stay inside these ranges and needn't reach their ends.
Inputs may be any that keep to these rules, and one draw needn't show every extreme that they name: `expert_ids`: each row names 4 different experts. Among the rows of one device, each expert below 4 is named by at most 32 rows, and one of them by exactly 32 rows on every device.
All inputs are finite; a program needn't handle non-finite values. No bound on the sum of `guard_mask` on one device may be relied on, other than what follows from the above.
Results may differ from the reference program's by a relative error of at most 0.0057.
Values may be sent and summed in bfloat16 or wider, within the bound.
A program may use at most 128 MiB of HBM per device.

```python
import jax
import jax.numpy as jnp
from jax import lax

D = 2880
HIDDEN_SIZE = 2880
EXPERTS = 128
TOP = 4
EXP_WIN = 4
TOK_DEV = 128
CAP = 32
TOKENS = 65536
COLS = 16384


def draw_expert_ids(key, part):
    key = jax.random.fold_in(key, 7)
    k_hot, k_count, k_rank, k_other, k_order = jax.random.split(key, 5)
    blocks = TOKENS // TOK_DEV
    hot = jax.random.randint(k_hot, (), 0, EXP_WIN)
    counts = jax.random.randint(k_count, (blocks, EXP_WIN), CAP // 4, CAP + 1)
    counts = jnp.where(jnp.arange(EXP_WIN)[None, :] == hot, CAP, counts)
    rank_keys = jax.random.randint(k_rank, (blocks, EXP_WIN, TOK_DEV), 0, 2 ** 20) * TOK_DEV + jnp.arange(TOK_DEV)[None, None, :]
    rank = jnp.argsort(jnp.argsort(rank_keys, axis=2), axis=2)
    chosen = jnp.transpose(rank < counts[:, :, None], (0, 2, 1))
    rest = EXPERTS - EXP_WIN
    other_keys = jax.random.randint(k_other, (blocks, TOK_DEV, rest), 0, 2 ** 20) * rest + jnp.arange(rest)[None, None, :]
    values, other = lax.top_k(other_keys, TOP)
    other = other + EXP_WIN
    filler = jnp.zeros((blocks, TOK_DEV, TOP - EXP_WIN), dtype=bool)
    chosen_full = jnp.concatenate([chosen, filler], axis=2)
    picked = jnp.where(chosen_full, jnp.arange(TOP)[None, None, :], other)
    order_keys = jax.random.randint(k_order, (blocks, TOK_DEV, TOP), 0, 2 ** 20) * TOP + jnp.arange(TOP)[None, None, :]
    order = jnp.argsort(order_keys, axis=2)
    picked = jnp.take_along_axis(picked, order, axis=2)
    return picked.reshape(TOKENS, TOP).astype(jnp.int32)


def with_ends(values, stream_key, least, top_value):
    dims = values.shape
    place = [jax.random.randint(jax.random.fold_in(stream_key, axis), (), 0, dims[axis]) for axis in range(len(dims))]
    values = values.at[tuple(place)].set(least)
    longest = dims.index(max(dims))
    place[longest] = (place[longest] + 1) % dims[longest]
    return values.at[tuple(place)].set(top_value)


def steps_of(own_key, shape, pieces, least, largest):
    gain = 1.0
    for position, parts in pieces:
        draws = jax.random.uniform(jax.random.fold_in(jax.random.fold_in(own_key, 6), position), (parts,), jnp.float32, least / len(pieces), largest / len(pieces))
        gain = gain * jnp.repeat(jnp.exp(draws), shape[position] // parts).reshape((-1,) + (1,) * (len(shape) - 1 - position))
    return gain


def bell_draw(key, shape, scale, bound, pieces=(), kind=jnp.bfloat16):
    array = scale * jax.random.normal(key, shape, jnp.float32)
    if pieces:
        array = array * steps_of(key, shape, pieces, -0.22, 0.18)
    return jnp.clip(array, -bound, bound).astype(kind)


def setup_inputs(seed: int = 0) -> dict:
    keys = jax.random.split(jax.random.key(seed), 7)
    upstream = bell_draw(keys[0], (TOKENS, D), 1.0, 6.0, ((0, 512),))
    router_logits = bell_draw(keys[1], (TOKENS, TOP), 1.0, 4.0, ((0, 512),), jnp.float32)
    expert_ids = draw_expert_ids(jax.random.fold_in(keys[6], 71), 0)
    guard_mask = with_ends((jax.random.randint(keys[3], (TOKENS,), 0, 8) < 7).astype(jnp.int32), jax.random.fold_in(keys[3], 1), 0, 1)
    w_down = bell_draw(keys[4], (EXP_WIN * HIDDEN_SIZE, D), HIDDEN_SIZE ** -0.5, 0.109375, ((0, 32),))
    saved_hidden = bell_draw(keys[5], (EXP_WIN * HIDDEN_SIZE, COLS), 0.1, 0.59765625, ((0, 32), (1, 16)))
    return dict(upstream=upstream, router_logits=router_logits, expert_ids=expert_ids, guard_mask=guard_mask, w_down=w_down, saved_hidden=saved_hidden)


def reference(upstream, router_logits, expert_ids, guard_mask, w_down, saved_hidden):
    tokens = upstream.shape[0]
    blocks = tokens // TOK_DEV
    cols_total = blocks * CAP
    probs = jax.nn.softmax(router_logits.astype(jnp.float32), axis=1)
    combine = lax.optimization_barrier(probs.astype(jnp.bfloat16)).astype(jnp.float32)
    live = (guard_mask[:, None] == 1) & (expert_ids < EXP_WIN)
    onehot = ((expert_ids[:, :, None] == jnp.arange(EXP_WIN, dtype=jnp.int32)[None, None, :]) & live[:, :, None]).astype(jnp.int32)
    flat = onehot.reshape(blocks, TOK_DEV * TOP, EXP_WIN)
    before = jnp.cumsum(flat, axis=1) - flat
    slot = jnp.sum(before * flat, axis=2).reshape(tokens, TOP)
    block_of = (jnp.arange(tokens, dtype=jnp.int32) // TOK_DEV)[:, None]
    column = (block_of * CAP + slot).astype(jnp.int32)

    def one_expert(expert):
        chosen = live & (expert_ids == expert)
        target = jnp.where(chosen, column, cols_total).astype(jnp.int32)
        rows = jnp.zeros((cols_total, D), jnp.bfloat16)
        weights = jnp.zeros((cols_total,), jnp.float32)
        for k in range(TOP):
            rows = rows.at[target[:, k]].set(upstream, mode="drop")
            weights = weights.at[target[:, k]].set(combine[:, k], mode="drop")
        start = (expert * HIDDEN_SIZE).astype(jnp.int32)
        w_part = lax.dynamic_slice_in_dim(w_down, start, HIDDEN_SIZE, 0)
        h_part = lax.dynamic_slice_in_dim(saved_hidden, start, HIDDEN_SIZE, 0).astype(jnp.float32)
        image = lax.dot_general(w_part, rows, (((1,), (1,)), ((), ())), preferred_element_type=jnp.float32)
        hidden_grad = (weights[None, :] * image).astype(jnp.bfloat16)
        inner = jnp.sum(h_part * image, axis=0)
        scaled = (weights[None, :] * h_part).astype(jnp.bfloat16)
        down_grad = lax.dot_general(rows, scaled, (((0,), (1,)), ((), ())), preferred_element_type=jnp.float32).astype(jnp.bfloat16)
        return hidden_grad, inner, down_grad

    hidden_all, inner_all, down_all = lax.map(one_expert, jnp.arange(EXP_WIN, dtype=jnp.int32))
    grad_hidden = hidden_all.reshape(EXP_WIN * HIDDEN_SIZE, cols_total)
    grad_down = jnp.transpose(down_all, (1, 0, 2)).reshape(D, EXP_WIN * HIDDEN_SIZE)
    safe_expert = jnp.clip(expert_ids, 0, EXP_WIN - 1).astype(jnp.int32)
    safe_column = jnp.clip(column, 0, cols_total - 1).astype(jnp.int32)
    dprob = jnp.where(live, inner_all[safe_expert, safe_column], 0.0)
    grad_logits = probs * (dprob - jnp.sum(probs * dprob, axis=1, keepdims=True))
    return grad_hidden, grad_down, grad_logits
```

```python
import functools

import jax
import jax.numpy as jnp
from jax import lax
from jax.experimental import pallas as pl
from jax.experimental.pallas import tpu as pltpu
from jax.sharding import PartitionSpec as P

MESH = pl.DeviceIdType.MESH
F32 = jnp.float32
BF16 = jnp.bfloat16

NE = 4
NX = 4
NJ = 8
NZ = 16
CAP = 32
TOK = 128
D = 2880
BLK = 180
PBLK = 192
NQ = 8
QW = 2 * PBLK
HID = 360
HPAD = 384
COLS = 1024
WLANE = BLK


def dot_nt(a, b):
    return lax.dot_general(a, b, (((1,), (1,)), ((), ())), preferred_element_type=F32)


def dot_nn(a, b):
    return lax.dot_general(a, b, (((1,), (0,)), ((), ())), preferred_element_type=F32)


def kernel(
    up_hbm, ids_ref, logits_ref, guard_ref, w_hbm, h_hbm,
    gh_hbm, gd_ref, gl_ref,
    up, upf, w, wq, h, scaled, rows, g, acc, gh, t_ref, sp, sm, rp, rm, sel, rs, rr, ri,
    in_sem, y_send, y_recv, x_send, xl_recv, xr_recv, xo_recv, s_send, s_recv,
    sp_send, rp_recv, sm_send, rm_recv, r1_send, r1_recv, r2_send, r2_recv, out_sem,
):
    z = lax.axis_index("dp")
    ep = lax.axis_index("ep")
    y = ep // NJ
    j = ep % NJ
    x = j // 2
    c = j % 2
    zr = lax.rem(z + 1, NZ)
    zl = lax.rem(z + NZ - 1, NZ)
    xr = lax.rem(x + 1, NX)
    xl = lax.rem(x + NX - 1, NX)
    xo = lax.rem(x + 2, NX)
    jr = xr * 2 + c
    jl = xl * 2 + c
    jo = xo * 2 + c
    js = x * 2 + (1 - c)
    half_z = z // 2

    cp_up = pltpu.make_async_copy(up_hbm, up, in_sem.at[0])
    cp_h = pltpu.make_async_copy(h_hbm, h, in_sem.at[1])
    cp_w = pltpu.make_async_copy(w_hbm, w, in_sem.at[2])
    cp_up.start()
    cp_h.start()
    cp_w.start()

    barrier = pltpu.get_barrier_semaphore()
    for d in range(1, NJ):
        pl.semaphore_signal(barrier, 1, device_id=(z, y * NJ + lax.rem(j + d, NJ)), device_id_type=MESH)
    for d in range(1, NE):
        pl.semaphore_signal(barrier, 1, device_id=(z, lax.rem(y + d, NE) * NJ + j), device_id_type=MESH)
    pl.semaphore_signal(barrier, 1, device_id=(zr, ep), device_id_type=MESH)
    pl.semaphore_signal(barrier, 1, device_id=(zl, ep), device_id_type=MESH)

    ids = ids_ref[...]
    logits = logits_ref[...]
    live = guard_ref[...] == 1
    top = jnp.max(logits, axis=0, keepdims=True)
    ex = jnp.exp(logits - top)
    probs = ex / jnp.sum(ex, axis=0, keepdims=True)
    combine = probs.astype(BF16).astype(F32)
    chosen = []
    weight = []
    for e in range(NE):
        hit = ((ids == e) & live).astype(F32)
        chosen.append(jnp.sum(hit, axis=0, keepdims=True))
        weight.append(jnp.sum(hit * combine, axis=0, keepdims=True))
    mask = jnp.concatenate(chosen + [jnp.zeros((8 - NE, TOK), F32)], axis=0)
    earlier = (
        lax.broadcasted_iota(jnp.int32, (TOK, TOK), 0) < lax.broadcasted_iota(jnp.int32, (TOK, TOK), 1)
    ).astype(F32).astype(BF16)
    slot = dot_nn(mask.astype(BF16), earlier)
    place = lax.broadcasted_iota(jnp.int32, (CAP, TOK), 0).astype(F32)
    picks = []
    wcols = []
    for e in range(NE):
        pick = jnp.where(slot[e:e + 1, :] == place, mask[e:e + 1, :], 0.0)
        picks.append(pick)
        wcols.append(jnp.sum(pick * weight[e], axis=1, keepdims=True))
    select = jnp.concatenate(picks, axis=0).astype(BF16)
    wcol = jnp.concatenate(wcols, axis=0)
    sel[...] = select
    at_weight = lax.broadcasted_iota(jnp.int32, (TOK, QW), 1) == WLANE

    cp_up.wait()
    upf[...] = up[...].astype(F32)
    gap = jnp.zeros((PBLK - BLK, TOK), F32)
    for q in range(NQ):
        a = q * 2 * BLK
        part = jnp.concatenate([upf[a:a + BLK, :], gap, upf[a + BLK:a + 2 * BLK, :], gap], axis=0)
        got = dot_nt(select, part.astype(BF16))
        rows[q] = jnp.where(at_weight, wcol, got).astype(BF16)

    def order(t):
        odd = lax.rem(t, 2)
        off = odd * ((t + 1) // 2) - (1 - odd) * (t // 2)
        return lax.rem(half_z + 4 + off + NQ, NQ)

    pl.semaphore_wait(barrier, NJ - 1 + NE - 1 + 2)

    def y_copy(t, d):
        q = order(t)
        e = lax.rem(y + d, NE)
        return pltpu.make_async_remote_copy(
            src_ref=rows.at[q, pl.ds(pl.multiple_of(e * CAP, CAP), CAP)],
            dst_ref=g.at[q, y, j],
            send_sem=y_send.at[t, d - 1],
            recv_sem=y_recv.at[t],
            device_id=(z, e * NJ + j),
            device_id_type=MESH,
        )

    def y_own(t):
        q = order(t)
        return pltpu.make_async_copy(
            rows.at[q, pl.ds(pl.multiple_of(y * CAP, CAP), CAP)], g.at[q, y, j], y_recv.at[t]
        )

    def x_copy(t, kind):
        q = order(t)
        src, to, sem = [
            (g.at[q, :, j], jr, xl_recv),
            (g.at[q, :, j], jl, xr_recv),
            (g.at[q, pl.ds(0, 2), jl], jr, xo_recv),
            (g.at[q, pl.ds(2, 2), jr], jl, xo_recv),
        ][kind]
        return pltpu.make_async_remote_copy(
            src_ref=src, dst_ref=src, send_sem=x_send.at[t, kind], recv_sem=sem.at[t],
            device_id=(z, y * NJ + to), device_id_type=MESH,
        )

    def s_copy(t, kind):
        q = order(t)
        piece = g.at[q, :, [j, jl, jr, jo][kind]]
        return pltpu.make_async_remote_copy(
            src_ref=piece, dst_ref=piece, send_sem=s_send.at[t, kind], recv_sem=s_recv.at[t],
            device_id=(z, y * NJ + js), device_id_type=MESH,
        )

    def wait_bytes(ref, sem):
        pltpu.make_async_copy(ref, ref, sem).wait()

    def start_y(t):
        y_own(t).start()
        for d in (2, 1, 3):
            y_copy(t, d).start()

    def own(t):
        wait_bytes(g.at[order(t), :, j], y_recv.at[t])
        x_copy(t, 0).start()
        x_copy(t, 1).start()
        s_copy(t, 0).start()

    def forward(t):
        q = order(t)
        wait_bytes(g.at[q, :, jl], xl_recv.at[t])
        x_copy(t, 2).start()
        s_copy(t, 1).start()
        wait_bytes(g.at[q, :, jr], xr_recv.at[t])
        x_copy(t, 3).start()
        s_copy(t, 2).start()

    def opposite(t):
        wait_bytes(g.at[order(t), :, jo], xo_recv.at[t])
        s_copy(t, 3).start()

    @pl.loop(0, NQ)
    def _(t):
        start_y(t)

    acc[...] = jnp.zeros_like(acc)
    cp_w.wait()
    wgap = jnp.zeros((HID, PBLK - BLK), BF16)
    for q in range(NQ):
        a = q * 2 * BLK
        wq[q] = jnp.concatenate([w[:, a:a + BLK], wgap, w[:, a + BLK:a + 2 * BLK], wgap], axis=1)

    own(0)
    own(1)
    forward(0)
    cp_h.wait()

    def plus_send(s):
        return pltpu.make_async_remote_copy(
            src_ref=sp.at[s], dst_ref=rp.at[s], send_sem=sp_send.at[s], recv_sem=rp_recv.at[s],
            device_id=(zr, ep), device_id_type=MESH,
        )

    def minus_send(s):
        return pltpu.make_async_remote_copy(
            src_ref=sm.at[s], dst_ref=rm.at[s], send_sem=sm_send.at[s], recv_sem=rm_recv.at[s],
            device_id=(zl, ep), device_id_type=MESH,
        )

    def plus(s):
        wait_bytes(rp.at[s - 1], rp_recv.at[s - 1])
        b = lax.rem(z + 8 - s + NZ, NZ)
        sp[s] = (t_ref[b] + rp[s - 1].astype(F32)).astype(BF16)
        plus_send(s).start()

    def minus(s):
        wait_bytes(rm.at[s - 1], rm_recv.at[s - 1])
        b = lax.rem(z + 9 + s, NZ)
        sm[s] = (t_ref[b] + rm[s - 1].astype(F32)).astype(BF16)
        minus_send(s).start()

    def column_weights(q):
        one = (lax.broadcasted_iota(jnp.int32, (8, 128), 1) == WLANE - 128).astype(F32).astype(BF16)
        tile = g[q, :, :, :, 128:256].reshape(COLS, 128)
        return dot_nt(one, tile)[0:1, :]

    @pl.loop(0, NQ)
    def _(t):
        q = order(t)

        @pl.when(t + 2 < NQ)
        def _():
            own(t + 2)

        @pl.when(t + 1 < NQ)
        def _():
            forward(t + 1)

        opposite(t)
        wait_bytes(g.at[q, :, pl.ds(0, 4)], s_recv.at[t])

        @pl.when(t == 0)
        def _():
            cw = column_weights(q)
            scaled[0:HID, :] = (cw * h[...].astype(F32)).astype(BF16)
            scaled[HID:HPAD, :] = jnp.zeros((HPAD - HID, COLS), BF16)

        part = dot_nn(scaled[...], g[q].reshape(COLS, QW)).T
        t_ref[2 * q] = part[0:PBLK]
        t_ref[2 * q + 1] = part[PBLK:QW]

        @pl.when(t == 0)
        def _():
            sp[0] = t_ref[lax.rem(z + 8, NZ)].astype(BF16)
            plus_send(0).start()

        @pl.when(t == 1)
        def _():
            sm[0] = t_ref[lax.rem(z + 9, NZ)].astype(BF16)
            minus_send(0).start()

        @pl.when(t >= 2)
        def _():
            plus(t - 1)
            minus(t - 1)

        for n in range(NE):
            acc[:, n * 256:(n + 1) * 256] += dot_nt(wq[q], g[q, n].reshape(256, QW))

    cw = column_weights(order(0))
    lane = lax.broadcasted_iota(jnp.int32, (1, 128), 1) // CAP
    sums = []
    for n in range(2 * NE):
        cols = slice(n * 128, (n + 1) * 128)
        image = acc[:, cols]
        sums.append(jnp.sum(h[:, cols].astype(F32) * image, axis=0, keepdims=True))
    table = jnp.concatenate(sums, axis=0)
    turned = [table] + [pltpu.roll(table, CAP * d, 1) for d in range(1, 4)]
    for i in range(NJ):
        line = jnp.zeros((1, 128), F32)
        for n in range(NE):
            src = turned[(n - i) % 4][2 * n + i // 4:2 * n + i // 4 + 1, :]
            line = jnp.where(lane == n, src, line)
        rs[i] = jnp.broadcast_to(line, (8, 128))
    rr[j] = rs[j]

    def r1(d):
        to = lax.rem(j + d, NJ)
        return pltpu.make_async_remote_copy(
            src_ref=rs.at[to], dst_ref=rr.at[j], send_sem=r1_send.at[d - 1], recv_sem=r1_recv.at[d - 1],
            device_id=(z, y * NJ + to), device_id_type=MESH,
        )

    for d in range(1, NJ):
        r1(d).start()

    gh[...] = (cw * acc[...]).astype(BF16)
    cp_gh = pltpu.make_async_copy(gh, gh_hbm, out_sem)
    cp_gh.start()

    plus(7)

    for d in range(1, NJ):
        r1(d).wait_recv()
    total = rr[0]
    for i in range(1, NJ):
        total = total + rr[i]
    ri[y] = total

    def r2(d):
        to = lax.rem(y + d, NE)
        return pltpu.make_async_remote_copy(
            src_ref=ri.at[y], dst_ref=ri.at[y], send_sem=r2_send.at[d - 1], recv_sem=r2_recv.at[d - 1],
            device_id=(z, to * NJ + j), device_id_type=MESH,
        )

    for d in range(1, NE):
        r2(d).start()

    wait_bytes(rm.at[6], rm_recv.at[6])
    partial = t_ref[z] + rm[6].astype(F32)

    for d in range(1, NE):
        r2(d).wait_recv()
    lanes = lax.broadcasted_iota(jnp.int32, (8, 128), 1) // CAP
    subl = lax.broadcasted_iota(jnp.int32, (8, 128), 0)
    inner = jnp.zeros((8, 128), F32)
    for e in range(NE):
        moved = pltpu.roll(ri[e], lax.rem(CAP * (e + NE - y), 128), 1)
        inner = jnp.where((lanes == e) & (subl == e), moved, inner)
    hi = inner.astype(BF16)
    rest = inner - hi.astype(F32)
    mid = rest.astype(BF16)
    low = (rest - mid.astype(F32)).astype(BF16)
    selected = sel[...]
    found = dot_nn(hi, selected) + dot_nn(mid, selected) + dot_nn(low, selected)
    dprob = jnp.zeros((4, TOK), F32)
    for e in range(NE):
        dprob = dprob + jnp.where((ids == e) & live, found[e:e + 1, :], 0.0)
    gl_ref[...] = probs * (dprob - jnp.sum(probs * dprob, axis=0, keepdims=True))

    wait_bytes(rp.at[7], rp_recv.at[7])
    final = partial + rp[7].astype(F32)
    gd_ref[...] = final[0:BLK, 0:HID].astype(BF16)

    @pl.loop(0, NQ)
    def _(t):
        for d in range(1, NE):
            y_copy(t, d).wait_send()
        for kind in range(4):
            x_copy(t, kind).wait_send()
            s_copy(t, kind).wait_send()
        plus_send(t).wait_send()

    @pl.loop(0, NQ - 1)
    def _(t):
        minus_send(t).wait_send()

    for d in range(1, NJ):
        r1(d).wait_send()
    for d in range(1, NE):
        r2(d).wait_send()
    cp_gh.wait()


def body(upstream, router_logits, expert_ids, guard_mask, w_down, saved_hidden):
    dma = pltpu.SemaphoreType.DMA
    vmem = pl.BlockSpec(memory_space=pltpu.VMEM)
    anywhere = pl.BlockSpec(memory_space=pl.ANY)
    gh, gd, gl = pl.pallas_call(
        kernel,
        out_shape=(
            jax.ShapeDtypeStruct((HID, COLS), BF16),
            jax.ShapeDtypeStruct((BLK, HID), BF16),
            jax.ShapeDtypeStruct((4, TOK), F32),
        ),
        in_specs=[anywhere, vmem, vmem, vmem, anywhere, anywhere],
        out_specs=(anywhere, vmem, vmem),
        scratch_shapes=[
            pltpu.VMEM((D, TOK), BF16),
            pltpu.VMEM((D, TOK), F32),
            pltpu.VMEM((HID, D), BF16),
            pltpu.VMEM((NQ, HID, QW), BF16),
            pltpu.VMEM((HID, COLS), BF16),
            pltpu.VMEM((HPAD, COLS), BF16),
            pltpu.VMEM((NQ, TOK, QW), BF16),
            pltpu.VMEM((NQ, NE, NJ, CAP, QW), BF16),
            pltpu.VMEM((HID, COLS), F32),
            pltpu.VMEM((HID, COLS), BF16),
            pltpu.VMEM((NZ, PBLK, HPAD), F32),
            pltpu.VMEM((8, PBLK, HPAD), BF16),
            pltpu.VMEM((8, PBLK, HPAD), BF16),
            pltpu.VMEM((8, PBLK, HPAD), BF16),
            pltpu.VMEM((8, PBLK, HPAD), BF16),
            pltpu.VMEM((TOK, TOK), BF16),
            pltpu.VMEM((NJ, 8, 128), F32),
            pltpu.VMEM((NJ, 8, 128), F32),
            pltpu.VMEM((NE, 8, 128), F32),
            dma((3,)),
            dma((NQ, 3)), dma((NQ,)),
            dma((NQ, 4)), dma((NQ,)), dma((NQ,)), dma((NQ,)),
            dma((NQ, 4)), dma((NQ,)),
            dma((8,)), dma((8,)), dma((8,)), dma((8,)),
            dma((7,)), dma((7,)), dma((3,)), dma((3,)),
            dma,
        ],
        compiler_params=pltpu.CompilerParams(
            collective_id=0, has_side_effects=True, vmem_limit_bytes=50 * 1024 * 1024
        ),
    )(upstream.T, expert_ids.T, router_logits.T, guard_mask.reshape(1, TOK), w_down, saved_hidden)
    return gh, gd, gl.T


def solution(mesh):
    in_specs = (
        P(("dp", "ep"), None),
        P(("dp", "ep"), None),
        P(("dp", "ep"), None),
        P(("dp", "ep")),
        P("ep", None),
        P("ep", "dp"),
    )
    out_specs = (P("ep", "dp"), P("dp", "ep"), P(("dp", "ep"), None))
    return jax.shard_map(body, mesh=mesh, in_specs=in_specs, out_specs=out_specs, check_vma=False)
```

```python
import jax
import jax.numpy as jnp
from jax import lax
from jax.experimental import pallas as pl
from jax.experimental.pallas import tpu as pltpu
from jax.sharding import PartitionSpec as P

MESH = pl.DeviceIdType.MESH
F32 = jnp.float32
BF16 = jnp.bfloat16

NE = 4
NX = 4
NJ = 8
NZ = 16
CAP = 32
TOK = 128
D = 2880
BLK = 180
PBLK = 192
NQ = 8
QW = 2 * PBLK
HID = 360
HPAD = 384
COLS = 1024
HALF = PBLK // 2
WLANE = BLK


def dot_nt(a, b):
    return lax.dot_general(a, b, (((1,), (1,)), ((), ())), preferred_element_type=F32)


def dot_nn(a, b):
    return lax.dot_general(a, b, (((1,), (0,)), ((), ())), preferred_element_type=F32)


def kernel(
    up_hbm, ids_hbm, logits_hbm, guard_hbm, w_hbm, h_hbm,
    gh_hbm, gd_hbm, gl_hbm,
    ids_ref, logits_ref, guard_ref, gd, gl, up, upf, upb, w, wblk, wq, h, scaled, cws, rows, g, acc, gh,
    t_ref, sp, sm, rp, rm, sel, rs, rr, ri,
    in_sem, y_send, y_recv, x_send, xl_recv, xr_recv, xo_recv, s_send, s_recv,
    sp_send, rp_recv, sm_send, rm_recv, r1_send, r1_recv, r2_send, r2_recv, out_sem,
):
    z = lax.axis_index("dp")
    ep = lax.axis_index("ep")
    y = ep // NJ
    j = ep % NJ
    x = j // 2
    c = j % 2
    zr = lax.rem(z + 1, NZ)
    zl = lax.rem(z + NZ - 1, NZ)
    jr = lax.rem(x + 1, NX) * 2 + c
    jl = lax.rem(x + NX - 1, NX) * 2 + c
    jo = lax.rem(x + 2, NX) * 2 + c
    js = x * 2 + (1 - c)

    cp_small = [
        pltpu.make_async_copy(ids_hbm, ids_ref, in_sem.at[3]),
        pltpu.make_async_copy(logits_hbm, logits_ref, in_sem.at[4]),
        pltpu.make_async_copy(guard_hbm, guard_ref, in_sem.at[5]),
    ]
    cp_up = pltpu.make_async_copy(up_hbm, up, in_sem.at[0])
    cp_h = pltpu.make_async_copy(h_hbm, h, in_sem.at[1])
    cp_w = pltpu.make_async_copy(w_hbm, w, in_sem.at[2])
    for cp in cp_small:
        cp.start()
    cp_up.start()
    cp_w.start()
    cp_h.start()

    barrier = pltpu.get_barrier_semaphore()
    for d in range(1, NJ):
        pl.semaphore_signal(barrier, 1, device_id=(z, y * NJ + lax.rem(j + d, NJ)), device_id_type=MESH)
    for d in range(1, NE):
        pl.semaphore_signal(barrier, 1, device_id=(z, lax.rem(y + d, NE) * NJ + j), device_id_type=MESH)
    pl.semaphore_signal(barrier, 1, device_id=(zr, ep), device_id_type=MESH)
    pl.semaphore_signal(barrier, 1, device_id=(zl, ep), device_id_type=MESH)

    for cp in cp_small:
        cp.wait()
    ids = ids_ref[...]
    logits = logits_ref[...]
    live = guard_ref[...] == 1
    top = jnp.max(logits, axis=0, keepdims=True)
    ex = jnp.exp(logits - top)
    probs = ex / jnp.sum(ex, axis=0, keepdims=True)
    combine = probs.astype(BF16).astype(F32)
    chosen = []
    weight = []
    for e in range(NE):
        hit = ((ids == e) & live).astype(F32)
        chosen.append(jnp.sum(hit, axis=0, keepdims=True))
        weight.append(jnp.sum(hit * combine, axis=0, keepdims=True))
    mask = jnp.concatenate(chosen + [jnp.zeros((8 - NE, TOK), F32)], axis=0)
    earlier = (
        lax.broadcasted_iota(jnp.int32, (TOK, TOK), 0) < lax.broadcasted_iota(jnp.int32, (TOK, TOK), 1)
    ).astype(F32).astype(BF16)
    slot = dot_nn(mask.astype(BF16), earlier)
    place = lax.broadcasted_iota(jnp.int32, (CAP, TOK), 0).astype(F32)
    picks = []
    wcols = []
    for e in range(NE):
        pick = jnp.where(slot[e:e + 1, :] == place, mask[e:e + 1, :], 0.0)
        picks.append(pick)
        wcols.append(jnp.sum(pick * weight[e], axis=1, keepdims=True))
    select = jnp.concatenate(picks, axis=0).astype(BF16)
    wcol = jnp.concatenate(wcols, axis=0)
    sel[...] = select
    at_weight = lax.broadcasted_iota(jnp.int32, (TOK, QW), 1) == WLANE

    cp_up.wait()
    upf[...] = up[...].astype(F32)
    gap = jnp.zeros((PBLK - BLK, TOK), F32)
    for b in range(NZ):
        upb[b] = jnp.concatenate([upf[b * BLK:(b + 1) * BLK, :], gap], axis=0).astype(BF16)

    def first(t):
        return lax.rem(z + 8 - t + NZ, NZ)

    def second(t):
        return lax.rem(z + 9 + t, NZ)

    def make_rows(t):
        part = jnp.concatenate([upb[first(t)], upb[second(t)]], axis=0)
        got = dot_nt(sel[...], part)
        rows[t] = jnp.where(at_weight, wcol, got).astype(BF16)
        g[t, 0, j] = rows[t, pl.ds(pl.multiple_of(y * CAP, CAP), CAP), :]

    def y_copy(t, d):
        e = lax.rem(y + d, NE)
        return pltpu.make_async_remote_copy(
            src_ref=rows.at[t, pl.ds(pl.multiple_of(e * CAP, CAP), CAP)],
            dst_ref=g.at[t, NE - d, j],
            send_sem=y_send.at[t, d - 1],
            recv_sem=y_recv.at[t],
            device_id=(z, e * NJ + j),
            device_id_type=MESH,
        )

    def x_copy(t, kind):
        ref, to, sem = [
            (g.at[t, 0, j], jr, xl_recv),
            (g.at[t, 0, j], jl, xr_recv),
            (g.at[t, pl.ds(1, 3), j], jr, xl_recv),
            (g.at[t, pl.ds(1, 3), j], jl, xr_recv),
            (g.at[t, pl.ds(0, 2), jl], jr, xo_recv),
            (g.at[t, pl.ds(2, 2), jr], jl, xo_recv),
        ][kind]
        return pltpu.make_async_remote_copy(
            src_ref=ref, dst_ref=ref, send_sem=x_send.at[t, kind], recv_sem=sem.at[t],
            device_id=(z, y * NJ + to), device_id_type=MESH,
        )

    def s_copy(t, kind):
        ref = [
            g.at[t, 0, j],
            g.at[t, pl.ds(1, 3), j],
            g.at[t, :, jl],
            g.at[t, :, jr],
            g.at[t, :, jo],
        ][kind]
        return pltpu.make_async_remote_copy(
            src_ref=ref, dst_ref=ref, send_sem=s_send.at[t, kind], recv_sem=s_recv.at[t],
            device_id=(z, y * NJ + js), device_id_type=MESH,
        )

    def wait_bytes(ref, sem):
        pltpu.make_async_copy(ref, ref, sem).wait()

    def start(t):
        for d in (2, 1, 3):
            y_copy(t, d).start()
        x_copy(t, 0).start()
        x_copy(t, 1).start()
        s_copy(t, 0).start()

    def rest(t):
        wait_bytes(g.at[t, pl.ds(1, 3), j], y_recv.at[t])
        x_copy(t, 2).start()
        x_copy(t, 3).start()
        s_copy(t, 1).start()

    def forward(t):
        wait_bytes(g.at[t, :, jl], xl_recv.at[t])
        x_copy(t, 4).start()
        s_copy(t, 2).start()
        wait_bytes(g.at[t, :, jr], xr_recv.at[t])
        x_copy(t, 5).start()
        s_copy(t, 3).start()

    def opposite(t):
        wait_bytes(g.at[t, :, jo], xo_recv.at[t])
        s_copy(t, 4).start()

    make_rows(0)
    pl.semaphore_wait(barrier, NJ - 1 + NE - 1 + 2)
    start(0)
    make_rows(1)
    start(1)
    make_rows(2)
    start(2)

    cp_w.wait()
    wgap = jnp.zeros((HID, PBLK - BLK), BF16)
    for b in range(NZ):
        wblk[b] = jnp.concatenate([w[:, b * BLK:(b + 1) * BLK], wgap], axis=1)

    def pair_w(t):
        wq[t] = jnp.concatenate([wblk[first(t)], wblk[second(t)]], axis=1)

    pair_w(0)
    rest(0)
    make_rows(3)
    start(3)
    rest(1)
    acc[...] = jnp.zeros_like(acc)
    pair_w(1)
    forward(0)
    make_rows(4)
    start(4)
    rest(2)
    cp_h.wait()
    forward(1)

    def plus_send(t, half):
        at = pl.ds(half * HALF, HALF)
        return pltpu.make_async_remote_copy(
            src_ref=sp.at[t, at], dst_ref=rp.at[t, at], send_sem=sp_send.at[t, half], recv_sem=rp_recv.at[t, half],
            device_id=(zr, ep), device_id_type=MESH,
        )

    def minus_send(t, half):
        at = pl.ds(half * HALF, HALF)
        return pltpu.make_async_remote_copy(
            src_ref=sm.at[t, at], dst_ref=rm.at[t, at], send_sem=sm_send.at[t, half], recv_sem=rm_recv.at[t, half],
            device_id=(zl, ep), device_id_type=MESH,
        )

    def chains(t, half):
        at = slice(half * HALF, (half + 1) * HALF)

        @pl.when(t == 0)
        def _():
            sp[t, at, :] = t_ref[at, :].astype(BF16)
            sm[t, at, :] = t_ref[PBLK + at.start:PBLK + at.stop, :].astype(BF16)

        @pl.when(t > 0)
        def _():
            ref = rp.at[t - 1, pl.ds(half * HALF, HALF)]
            wait_bytes(ref, rp_recv.at[t - 1, half])
            sp[t, at, :] = (t_ref[at, :] + rp[t - 1, at, :].astype(F32)).astype(BF16)

        plus_send(t, half).start()

        @pl.when((t > 0) & (t < NQ - 1))
        def _():
            ref = rm.at[t - 1, pl.ds(half * HALF, HALF)]
            wait_bytes(ref, rm_recv.at[t - 1, half])
            sm[t, at, :] = (t_ref[PBLK + at.start:PBLK + at.stop, :] + rm[t - 1, at, :].astype(F32)).astype(BF16)

        @pl.when(t < NQ - 1)
        def _():
            minus_send(t, half).start()

    def source(n):
        return lax.rem(n - y + NE, NE)

    def scale_columns():
        one = (lax.broadcasted_iota(jnp.int32, (8, 128), 1) == WLANE - 128).astype(F32).astype(BF16)
        for n in range(NE):
            dy = source(n)
            cols = slice(n * 256, (n + 1) * 256)
            cw = dot_nt(one, g[0, dy, :, :, 128:256].reshape(256, 128))
            cws[:, cols] = cw
            scaled[dy, 0:HID, :] = (cw[0:1, :] * h[:, cols].astype(F32)).astype(BF16)
            scaled[dy, HID:HPAD, :] = jnp.zeros((HPAD - HID, 256), BF16)

    def r1(d):
        to = lax.rem(j + d, NJ)
        return pltpu.make_async_remote_copy(
            src_ref=rs.at[to], dst_ref=rr.at[j], send_sem=r1_send.at[d - 1], recv_sem=r1_recv.at[d - 1],
            device_id=(z, y * NJ + to), device_id_type=MESH,
        )

    def inner_products():
        lane = lax.broadcasted_iota(jnp.int32, (1, 128), 1) // CAP
        sums = []
        for n in range(2 * NE):
            cols = slice(n * 128, (n + 1) * 128)
            sums.append(jnp.sum(h[:, cols].astype(F32) * acc[:, cols], axis=0, keepdims=True))
        table = jnp.concatenate(sums, axis=0)
        turned = [table] + [pltpu.roll(table, CAP * d, 1) for d in range(1, 4)]
        for i in range(NJ):
            line = jnp.zeros((1, 128), F32)
            for n in range(NE):
                src = turned[(n - i) % 4][2 * n + i // 4:2 * n + i // 4 + 1, :]
                line = jnp.where(lane == n, src, line)
            rs[i] = jnp.broadcast_to(line, (8, 128))
        for d in range(1, NJ):
            r1(d).start()
        rr[j] = rs[j]

    @pl.loop(0, NQ)
    def _(t):
        opposite(t)

        @pl.when(t + 5 < NQ)
        def _():
            make_rows(t + 5)
            start(t + 5)

        @pl.when(t + 3 < NQ)
        def _():
            rest(t + 3)

        @pl.when(t + 2 < NQ)
        def _():
            pair_w(t + 2)
            forward(t + 2)

        @pl.when(t > 0)
        def _():
            chains(t - 1, 1)

        wait_bytes(g.at[t, :, pl.ds(0, 4)], s_recv.at[t])

        @pl.when(t == 0)
        def _():
            scale_columns()

        for n in range(NE):
            acc[:, n * 256:(n + 1) * 256] += dot_nt(wq[t], g[t, source(n)].reshape(256, QW))

        @pl.when(t == NQ - 1)
        def _():
            inner_products()

        part = dot_nn(scaled[0], g[t, 0].reshape(256, QW))
        for dy in range(1, NE):
            part = part + dot_nn(scaled[dy], g[t, dy].reshape(256, QW))
        t_ref[...] = part.T
        chains(t, 0)

    chains(NQ - 1, 1)

    gh[...] = (cws[0:1, :] * acc[...]).astype(BF16)
    cp_gh = pltpu.make_async_copy(gh, gh_hbm, out_sem.at[0])
    cp_gh.start()

    for d in range(1, NJ):
        r1(d).wait_recv()
    total = rr[0]
    for i in range(1, NJ):
        total = total + rr[i]
    ri[y] = total

    def r2(d):
        to = lax.rem(y + d, NE)
        return pltpu.make_async_remote_copy(
            src_ref=ri.at[y], dst_ref=ri.at[y], send_sem=r2_send.at[d - 1], recv_sem=r2_recv.at[d - 1],
            device_id=(z, to * NJ + j), device_id_type=MESH,
        )

    for d in range(1, NE):
        r2(d).start()

    @pl.loop(0, NQ)
    def _(t):
        for d in range(1, NE):
            y_copy(t, d).wait_send()
        for kind in range(6):
            x_copy(t, kind).wait_send()
        for kind in range(5):
            s_copy(t, kind).wait_send()

    for half in range(2):
        wait_bytes(rm.at[NQ - 2, pl.ds(half * HALF, HALF)], rm_recv.at[NQ - 2, half])
    t_ref[0:PBLK, :] = t_ref[PBLK:QW, :] + rm[NQ - 2].astype(F32)

    for d in range(1, NE):
        r2(d).wait_recv()
    lanes = lax.broadcasted_iota(jnp.int32, (8, 128), 1) // CAP
    subl = lax.broadcasted_iota(jnp.int32, (8, 128), 0)
    inner = jnp.zeros((8, 128), F32)
    for e in range(NE):
        moved = pltpu.roll(ri[e], lax.rem(CAP * (e + NE - y), 128), 1)
        inner = jnp.where((lanes == e) & (subl == e), moved, inner)
    hi = inner.astype(BF16)
    rem = inner - hi.astype(F32)
    mid = rem.astype(BF16)
    low = (rem - mid.astype(F32)).astype(BF16)
    selected = sel[...]
    found = dot_nn(hi, selected) + dot_nn(mid, selected) + dot_nn(low, selected)
    dprob = jnp.zeros((4, TOK), F32)
    for e in range(NE):
        dprob = dprob + jnp.where((ids == e) & live, found[e:e + 1, :], 0.0)
    gl[...] = probs * (dprob - jnp.sum(probs * dprob, axis=0, keepdims=True))
    cp_gl = pltpu.make_async_copy(gl, gl_hbm, out_sem.at[1])
    cp_gl.start()

    for half in range(2):
        wait_bytes(rp.at[NQ - 1, pl.ds(half * HALF, HALF)], rp_recv.at[NQ - 1, half])
    final = t_ref[0:PBLK, :] + rp[NQ - 1].astype(F32)
    gd[...] = final[0:BLK, 0:HID].astype(BF16)
    cp_gd = pltpu.make_async_copy(gd, gd_hbm, out_sem.at[2])
    cp_gd.start()

    @pl.loop(0, NQ - 1)
    def _(t):
        for half in range(2):
            plus_send(t, half).wait_send()
            minus_send(t, half).wait_send()

    for half in range(2):
        plus_send(NQ - 1, half).wait_send()
    for d in range(1, NJ):
        r1(d).wait_send()
    for d in range(1, NE):
        r2(d).wait_send()
    cp_gh.wait()
    cp_gl.wait()
    cp_gd.wait()


def hand_over(gh_in, gd_in, gl_in, gh_out, gd_out, gl_out, gh, gd, gl, sem):
    refs = [(gh_in, gh, gh_out), (gd_in, gd, gd_out), (gl_in, gl, gl_out)]
    for i, (a, b, _) in enumerate(refs):
        pltpu.make_async_copy(a, b, sem.at[0, i]).start()
    for i, (a, b, o) in enumerate(refs):
        pltpu.make_async_copy(a, b, sem.at[0, i]).wait()
        pltpu.make_async_copy(b, o, sem.at[1, i]).start()
    for i, (_, b, o) in enumerate(refs):
        pltpu.make_async_copy(b, o, sem.at[1, i]).wait()


def body(upstream, router_logits, expert_ids, guard_mask, w_down, saved_hidden):
    dma = pltpu.SemaphoreType.DMA
    hbm = pl.BlockSpec(memory_space=pltpu.HBM)
    outs = (
        jax.ShapeDtypeStruct((HID, COLS), BF16),
        jax.ShapeDtypeStruct((BLK, HID), BF16),
        jax.ShapeDtypeStruct((4, TOK), F32),
    )
    results = pl.pallas_call(
        kernel,
        out_shape=outs,
        in_specs=[hbm] * 6,
        out_specs=(hbm, hbm, hbm),
        scratch_shapes=[
            pltpu.VMEM((4, TOK), jnp.int32),
            pltpu.VMEM((4, TOK), F32),
            pltpu.VMEM((1, TOK), jnp.int32),
            pltpu.VMEM((BLK, HID), BF16),
            pltpu.VMEM((4, TOK), F32),
            pltpu.VMEM((D, TOK), BF16),
            pltpu.VMEM((D, TOK), F32),
            pltpu.VMEM((NZ, PBLK, TOK), BF16),
            pltpu.VMEM((HID, D), BF16),
            pltpu.VMEM((NZ, HID, PBLK), BF16),
            pltpu.VMEM((NQ, HID, QW), BF16),
            pltpu.VMEM((HID, COLS), BF16),
            pltpu.VMEM((NE, HPAD, 256), BF16),
            pltpu.VMEM((8, COLS), F32),
            pltpu.VMEM((NQ, TOK, QW), BF16),
            pltpu.VMEM((NQ, NE, NJ, CAP, QW), BF16),
            pltpu.VMEM((HID, COLS), F32),
            pltpu.VMEM((HID, COLS), BF16),
            pltpu.VMEM((QW, HPAD), F32),
            pltpu.VMEM((NQ, PBLK, HPAD), BF16),
            pltpu.VMEM((NQ, PBLK, HPAD), BF16),
            pltpu.VMEM((NQ, PBLK, HPAD), BF16),
            pltpu.VMEM((NQ, PBLK, HPAD), BF16),
            pltpu.VMEM((TOK, TOK), BF16),
            pltpu.VMEM((NJ, 8, 128), F32),
            pltpu.VMEM((NJ, 8, 128), F32),
            pltpu.VMEM((NE, 8, 128), F32),
            dma((6,)),
            dma((NQ, 3)), dma((NQ,)),
            dma((NQ, 6)), dma((NQ,)), dma((NQ,)), dma((NQ,)),
            dma((NQ, 5)), dma((NQ,)),
            dma((NQ, 2)), dma((NQ, 2)), dma((NQ, 2)), dma((NQ, 2)),
            dma((7,)), dma((7,)), dma((3,)), dma((3,)),
            dma((3,)),
        ],
        compiler_params=pltpu.CompilerParams(
            collective_id=0, has_side_effects=True, vmem_limit_bytes=64 * 1024 * 1024
        ),
    )(upstream.T, expert_ids.T, router_logits.T, guard_mask.reshape(1, TOK), w_down, saved_hidden)
    gh, gd, gl = pl.pallas_call(
        hand_over,
        out_shape=outs,
        in_specs=[hbm] * 3,
        out_specs=(hbm, hbm, hbm),
        scratch_shapes=[
            pltpu.VMEM((HID, COLS), BF16),
            pltpu.VMEM((BLK, HID), BF16),
            pltpu.VMEM((4, TOK), F32),
            dma((2, 3)),
        ],
        compiler_params=pltpu.CompilerParams(vmem_limit_bytes=64 * 1024 * 1024),
    )(*results)
    return gh, gd, gl.T


def solution(mesh):
    in_specs = (
        P(("dp", "ep"), None),
        P(("dp", "ep"), None),
        P(("dp", "ep"), None),
        P(("dp", "ep")),
        P("ep", None),
        P("ep", "dp"),
    )
    out_specs = (P("ep", "dp"), P("dp", "ep"), P(("dp", "ep"), None))
    return jax.shard_map(body, mesh=mesh, in_specs=in_specs, out_specs=out_specs, check_vma=False)
```

```python
import jax
import jax.numpy as jnp
from jax import lax
from jax.experimental import pallas as pl
from jax.experimental.pallas import tpu as pltpu
from jax.sharding import PartitionSpec as P

MESH = pl.DeviceIdType.MESH
F32 = jnp.float32
BF16 = jnp.bfloat16

NE = 4
NX = 4
NJ = 8
NZ = 16
CAP = 32
TOK = 128
D = 2880
BLK = 180
PBLK = 192
NQ = 8
QW = 2 * PBLK
HID = 360
HPAD = 384
COLS = 1024
CUTS = 4
PART = PBLK // CUTS
WLANE = BLK


def dot_nt(a, b):
    return lax.dot_general(a, b, (((1,), (1,)), ((), ())), preferred_element_type=F32)


def dot_nn(a, b):
    return lax.dot_general(a, b, (((1,), (0,)), ((), ())), preferred_element_type=F32)


def kernel(
    up_hbm, ids_hbm, logits_hbm, guard_hbm, w_hbm, h_hbm,
    gh, gd, gl,
    ids_ref, logits_ref, guard_ref, up, upf, upb, w, wblk, wq, h, scaled, cws, rows, g, acc,
    t_ref, sp, sm, rp, rm, sel, rs, rr, ri,
    in_sem, y_send, y_recv, x_send, xl_recv, xr_recv, xo_recv, s_send, s_recv,
    sp_send, rp_recv, sm_send, rm_recv, r1_send, r1_recv, r2_send, r2_recv,
):
    z = lax.axis_index("dp")
    ep = lax.axis_index("ep")
    y = ep // NJ
    j = ep % NJ
    x = j // 2
    c = j % 2
    zr = lax.rem(z + 1, NZ)
    zl = lax.rem(z + NZ - 1, NZ)
    jr = lax.rem(x + 1, NX) * 2 + c
    jl = lax.rem(x + NX - 1, NX) * 2 + c
    jo = lax.rem(x + 2, NX) * 2 + c
    js = x * 2 + (1 - c)

    cp_small = [
        pltpu.make_async_copy(ids_hbm, ids_ref, in_sem.at[3]),
        pltpu.make_async_copy(logits_hbm, logits_ref, in_sem.at[4]),
        pltpu.make_async_copy(guard_hbm, guard_ref, in_sem.at[5]),
    ]
    cp_up = pltpu.make_async_copy(up_hbm, up, in_sem.at[0])
    cp_h = pltpu.make_async_copy(h_hbm, h, in_sem.at[1])
    cp_w = pltpu.make_async_copy(w_hbm, w, in_sem.at[2])
    for cp in cp_small:
        cp.start()
    cp_up.start()
    cp_w.start()
    cp_h.start()

    barrier = pltpu.get_barrier_semaphore()
    for d in range(1, NJ):
        pl.semaphore_signal(barrier, 1, device_id=(z, y * NJ + lax.rem(j + d, NJ)), device_id_type=MESH)
    for d in range(1, NE):
        pl.semaphore_signal(barrier, 1, device_id=(z, lax.rem(y + d, NE) * NJ + j), device_id_type=MESH)
    pl.semaphore_signal(barrier, 1, device_id=(zr, ep), device_id_type=MESH)
    pl.semaphore_signal(barrier, 1, device_id=(zl, ep), device_id_type=MESH)

    for cp in cp_small:
        cp.wait()
    ids = ids_ref[...]
    logits = logits_ref[...]
    live = guard_ref[...] == 1
    top = jnp.max(logits, axis=0, keepdims=True)
    ex = jnp.exp(logits - top)
    probs = ex / jnp.sum(ex, axis=0, keepdims=True)
    combine = probs.astype(BF16).astype(F32)
    chosen = []
    weight = []
    for e in range(NE):
        hit = ((ids == e) & live).astype(F32)
        chosen.append(jnp.sum(hit, axis=0, keepdims=True))
        weight.append(jnp.sum(hit * combine, axis=0, keepdims=True))
    mask = jnp.concatenate(chosen + [jnp.zeros((8 - NE, TOK), F32)], axis=0)
    earlier = (
        lax.broadcasted_iota(jnp.int32, (TOK, TOK), 0) < lax.broadcasted_iota(jnp.int32, (TOK, TOK), 1)
    ).astype(F32).astype(BF16)
    slot = dot_nn(mask.astype(BF16), earlier)
    place = lax.broadcasted_iota(jnp.int32, (CAP, TOK), 0).astype(F32)
    picks = []
    wcols = []
    for e in range(NE):
        pick = jnp.where(slot[e:e + 1, :] == place, mask[e:e + 1, :], 0.0)
        picks.append(pick)
        wcols.append(jnp.sum(pick * weight[e], axis=1, keepdims=True))
    select = jnp.concatenate(picks, axis=0).astype(BF16)
    wcol = jnp.concatenate(wcols, axis=0)
    sel[...] = select
    at_weight = lax.broadcasted_iota(jnp.int32, (TOK, QW), 1) == WLANE

    cp_up.wait()
    upf[...] = up[...].astype(F32)
    gap = jnp.zeros((PBLK - BLK, TOK), F32)
    for b in range(NZ):
        upb[b] = jnp.concatenate([upf[b * BLK:(b + 1) * BLK, :], gap], axis=0).astype(BF16)

    def first(t):
        return lax.rem(z + 8 - t + NZ, NZ)

    def second(t):
        return lax.rem(z + 9 + t, NZ)

    def make_rows(t):
        part = jnp.concatenate([upb[first(t)], upb[second(t)]], axis=0)
        got = dot_nt(sel[...], part)
        rows[t] = jnp.where(at_weight, wcol, got).astype(BF16)
        g[t, 0, j] = rows[t, pl.ds(pl.multiple_of(y * CAP, CAP), CAP), :]

    def y_copy(t, d):
        e = lax.rem(y + d, NE)
        return pltpu.make_async_remote_copy(
            src_ref=rows.at[t, pl.ds(pl.multiple_of(e * CAP, CAP), CAP)],
            dst_ref=g.at[t, NE - d, j],
            send_sem=y_send.at[t, d - 1],
            recv_sem=y_recv.at[t],
            device_id=(z, e * NJ + j),
            device_id_type=MESH,
        )

    def x_copy(t, kind):
        ref, to, sem = [
            (g.at[t, 0, j], jr, xl_recv),
            (g.at[t, 0, j], jl, xr_recv),
            (g.at[t, pl.ds(1, 3), j], jr, xl_recv),
            (g.at[t, pl.ds(1, 3), j], jl, xr_recv),
            (g.at[t, pl.ds(0, 2), jl], jr, xo_recv),
            (g.at[t, pl.ds(2, 2), jr], jl, xo_recv),
        ][kind]
        return pltpu.make_async_remote_copy(
            src_ref=ref, dst_ref=ref, send_sem=x_send.at[t, kind], recv_sem=sem.at[t],
            device_id=(z, y * NJ + to), device_id_type=MESH,
        )

    def s_copy(t, kind):
        ref = [
            g.at[t, 0, j],
            g.at[t, pl.ds(1, 3), j],
            g.at[t, :, jl],
            g.at[t, :, jr],
            g.at[t, :, jo],
        ][kind]
        return pltpu.make_async_remote_copy(
            src_ref=ref, dst_ref=ref, send_sem=s_send.at[t, kind], recv_sem=s_recv.at[t],
            device_id=(z, y * NJ + js), device_id_type=MESH,
        )

    def wait_bytes(ref, sem):
        pltpu.make_async_copy(ref, ref, sem).wait()

    def start(t):
        for d in (2, 1, 3):
            y_copy(t, d).start()
        x_copy(t, 0).start()
        x_copy(t, 1).start()
        s_copy(t, 0).start()

    def rest(t):
        wait_bytes(g.at[t, pl.ds(1, 3), j], y_recv.at[t])
        x_copy(t, 2).start()
        x_copy(t, 3).start()
        s_copy(t, 1).start()

    def forward(t):
        wait_bytes(g.at[t, :, jl], xl_recv.at[t])
        x_copy(t, 4).start()
        s_copy(t, 2).start()
        wait_bytes(g.at[t, :, jr], xr_recv.at[t])
        x_copy(t, 5).start()
        s_copy(t, 3).start()

    def opposite(t):
        wait_bytes(g.at[t, :, jo], xo_recv.at[t])
        s_copy(t, 4).start()

    make_rows(0)
    pl.semaphore_wait(barrier, NJ - 1 + NE - 1 + 2)
    start(0)
    make_rows(1)
    start(1)
    make_rows(2)
    start(2)

    cp_w.wait()
    wgap = jnp.zeros((HID, PBLK - BLK), BF16)
    for b in range(NZ):
        wblk[b] = jnp.concatenate([w[:, b * BLK:(b + 1) * BLK], wgap], axis=1)

    def pair_w(t):
        wq[t] = jnp.concatenate([wblk[first(t)], wblk[second(t)]], axis=1)

    pair_w(0)
    rest(0)
    make_rows(3)
    start(3)
    rest(1)
    acc[...] = jnp.zeros_like(acc)
    pair_w(1)
    forward(0)
    make_rows(4)
    start(4)
    rest(2)
    cp_h.wait()
    forward(1)

    def plus_send(t, k):
        at = pl.ds(k * PART, PART)
        return pltpu.make_async_remote_copy(
            src_ref=sp.at[t, at], dst_ref=rp.at[t, at], send_sem=sp_send.at[t, k], recv_sem=rp_recv.at[t, k],
            device_id=(zr, ep), device_id_type=MESH,
        )

    def minus_send(t, k):
        at = pl.ds(k * PART, PART)
        return pltpu.make_async_remote_copy(
            src_ref=sm.at[t, at], dst_ref=rm.at[t, at], send_sem=sm_send.at[t, k], recv_sem=rm_recv.at[t, k],
            device_id=(zl, ep), device_id_type=MESH,
        )

    def chains(t, k):
        at = slice(k * PART, (k + 1) * PART)
        at2 = slice(PBLK + k * PART, PBLK + (k + 1) * PART)

        @pl.when(t == 0)
        def _():
            sp[t, at, :] = t_ref[at, :].astype(BF16)
            plus_send(t, k).start()
            sm[t, at, :] = t_ref[at2, :].astype(BF16)
            minus_send(t, k).start()

        @pl.when(t > 0)
        def _():
            wait_bytes(rp.at[t - 1, pl.ds(k * PART, PART)], rp_recv.at[t - 1, k])
            sp[t, at, :] = (t_ref[at, :] + rp[t - 1, at, :].astype(F32)).astype(BF16)
            plus_send(t, k).start()

        @pl.when((t > 0) & (t < NQ - 1))
        def _():
            wait_bytes(rm.at[t - 1, pl.ds(k * PART, PART)], rm_recv.at[t - 1, k])
            sm[t, at, :] = (t_ref[at2, :] + rm[t - 1, at, :].astype(F32)).astype(BF16)
            minus_send(t, k).start()

    def source(n):
        return lax.rem(n - y + NE, NE)

    def scale_columns():
        one = (lax.broadcasted_iota(jnp.int32, (8, 128), 1) == WLANE - 128).astype(F32).astype(BF16)
        for n in range(NE):
            dy = source(n)
            cols = slice(n * 256, (n + 1) * 256)
            cw = dot_nt(one, g[0, dy, :, :, 128:256].reshape(256, 128))
            cws[:, cols] = cw
            scaled[dy, 0:HID, :] = (cw[0:1, :] * h[:, cols].astype(F32)).astype(BF16)
            scaled[dy, HID:HPAD, :] = jnp.zeros((HPAD - HID, 256), BF16)

    def r1(d):
        to = lax.rem(j + d, NJ)
        return pltpu.make_async_remote_copy(
            src_ref=rs.at[to], dst_ref=rr.at[j], send_sem=r1_send.at[d - 1], recv_sem=r1_recv.at[d - 1],
            device_id=(z, y * NJ + to), device_id_type=MESH,
        )

    def inner_products():
        lane = lax.broadcasted_iota(jnp.int32, (1, 128), 1) // CAP
        sums = []
        for n in range(2 * NE):
            cols = slice(n * 128, (n + 1) * 128)
            sums.append(jnp.sum(h[:, cols].astype(F32) * acc[:, cols], axis=0, keepdims=True))
        table = jnp.concatenate(sums, axis=0)
        turned = [table] + [pltpu.roll(table, CAP * d, 1) for d in range(1, 4)]
        for i in range(NJ):
            line = jnp.zeros((1, 128), F32)
            for n in range(NE):
                src = turned[(n - i) % 4][2 * n + i // 4:2 * n + i // 4 + 1, :]
                line = jnp.where(lane == n, src, line)
            rs[i] = jnp.broadcast_to(line, (8, 128))
        for d in range(1, NJ):
            r1(d).start()
        rr[j] = rs[j]

    @pl.loop(0, NQ)
    def _(t):
        opposite(t)

        @pl.when(t + 5 < NQ)
        def _():
            make_rows(t + 5)
            start(t + 5)

        @pl.when(t + 3 < NQ)
        def _():
            rest(t + 3)

        @pl.when(t > 0)
        def _():
            chains(t - 1, 1)

        @pl.when(t + 2 < NQ)
        def _():
            pair_w(t + 2)
            forward(t + 2)

        @pl.when(t > 0)
        def _():
            chains(t - 1, 2)

        wait_bytes(g.at[t, :, pl.ds(0, 4)], s_recv.at[t])

        @pl.when(t == 0)
        def _():
            scale_columns()

        for n in range(NE):
            acc[:, n * 256:(n + 1) * 256] += dot_nt(wq[t], g[t, source(n)].reshape(256, QW))

        @pl.when(t == NQ - 1)
        def _():
            inner_products()

        @pl.when(t > 0)
        def _():
            chains(t - 1, 3)

        part = dot_nn(scaled[0], g[t, 0].reshape(256, QW))
        for dy in range(1, NE):
            part = part + dot_nn(scaled[dy], g[t, dy].reshape(256, QW))
        t_ref[...] = part.T
        chains(t, 0)

    for k in range(1, CUTS):
        chains(NQ - 1, k)

    gh[...] = (cws[0:1, :] * acc[...]).astype(BF16)

    for d in range(1, NJ):
        r1(d).wait_recv()
    total = rr[0]
    for i in range(1, NJ):
        total = total + rr[i]
    ri[y] = total

    def r2(d):
        to = lax.rem(y + d, NE)
        return pltpu.make_async_remote_copy(
            src_ref=ri.at[y], dst_ref=ri.at[y], send_sem=r2_send.at[d - 1], recv_sem=r2_recv.at[d - 1],
            device_id=(z, to * NJ + j), device_id_type=MESH,
        )

    for d in range(1, NE):
        r2(d).start()

    @pl.loop(0, NQ)
    def _(t):
        for d in range(1, NE):
            y_copy(t, d).wait_send()
        for kind in range(6):
            x_copy(t, kind).wait_send()
        for kind in range(5):
            s_copy(t, kind).wait_send()

    for k in range(CUTS):
        wait_bytes(rm.at[NQ - 2, pl.ds(k * PART, PART)], rm_recv.at[NQ - 2, k])
    t_ref[0:PBLK, :] = t_ref[PBLK:QW, :] + rm[NQ - 2].astype(F32)

    for d in range(1, NE):
        r2(d).wait_recv()
    lanes = lax.broadcasted_iota(jnp.int32, (8, 128), 1) // CAP
    subl = lax.broadcasted_iota(jnp.int32, (8, 128), 0)
    inner = jnp.zeros((8, 128), F32)
    for e in range(NE):
        moved = pltpu.roll(ri[e], lax.rem(CAP * (e + NE - y), 128), 1)
        inner = jnp.where((lanes == e) & (subl == e), moved, inner)
    hi = inner.astype(BF16)
    rem = inner - hi.astype(F32)
    mid = rem.astype(BF16)
    low = (rem - mid.astype(F32)).astype(BF16)
    selected = sel[...]
    found = dot_nn(hi, selected) + dot_nn(mid, selected) + dot_nn(low, selected)
    dprob = jnp.zeros((4, TOK), F32)
    for e in range(NE):
        dprob = dprob + jnp.where((ids == e) & live, found[e:e + 1, :], 0.0)
    gl[...] = probs * (dprob - jnp.sum(probs * dprob, axis=0, keepdims=True))

    for k in range(CUTS):
        wait_bytes(rp.at[NQ - 1, pl.ds(k * PART, PART)], rp_recv.at[NQ - 1, k])
    final = t_ref[0:PBLK, :] + rp[NQ - 1].astype(F32)
    gd[...] = final[0:BLK, 0:HID].astype(BF16)

    @pl.loop(0, NQ - 1)
    def _(t):
        for k in range(CUTS):
            plus_send(t, k).wait_send()
            minus_send(t, k).wait_send()

    for k in range(CUTS):
        plus_send(NQ - 1, k).wait_send()
    for d in range(1, NJ):
        r1(d).wait_send()
    for d in range(1, NE):
        r2(d).wait_send()


def hand_over(gh_in, gd_in, gl_in, gh_out, gd_out, gl_out, sem):
    copies = [
        pltpu.make_async_copy(a, b, sem.at[i])
        for i, (a, b) in enumerate([(gh_in, gh_out), (gd_in, gd_out), (gl_in, gl_out)])
    ]
    for cp in copies:
        cp.start()
    for cp in copies:
        cp.wait()


def body(upstream, router_logits, expert_ids, guard_mask, w_down, saved_hidden):
    dma = pltpu.SemaphoreType.DMA
    vmem = pl.BlockSpec(memory_space=pltpu.VMEM)
    hbm = pl.BlockSpec(memory_space=pltpu.HBM)
    outs = (
        jax.ShapeDtypeStruct((HID, COLS), BF16),
        jax.ShapeDtypeStruct((BLK, HID), BF16),
        jax.ShapeDtypeStruct((4, TOK), F32),
    )
    results = pl.pallas_call(
        kernel,
        out_shape=(pltpu.VMEM((HID, COLS), BF16), pltpu.VMEM((BLK, HID), BF16), pltpu.VMEM((4, TOK), F32)),
        in_specs=[hbm] * 6,
        out_specs=(vmem, vmem, vmem),
        scratch_shapes=[
            pltpu.VMEM((4, TOK), jnp.int32),
            pltpu.VMEM((4, TOK), F32),
            pltpu.VMEM((1, TOK), jnp.int32),
            pltpu.VMEM((D, TOK), BF16),
            pltpu.VMEM((D, TOK), F32),
            pltpu.VMEM((NZ, PBLK, TOK), BF16),
            pltpu.VMEM((HID, D), BF16),
            pltpu.VMEM((NZ, HID, PBLK), BF16),
            pltpu.VMEM((NQ, HID, QW), BF16),
            pltpu.VMEM((HID, COLS), BF16),
            pltpu.VMEM((NE, HPAD, 256), BF16),
            pltpu.VMEM((8, COLS), F32),
            pltpu.VMEM((NQ, TOK, QW), BF16),
            pltpu.VMEM((NQ, NE, NJ, CAP, QW), BF16),
            pltpu.VMEM((HID, COLS), F32),
            pltpu.VMEM((QW, HPAD), F32),
            pltpu.VMEM((NQ, PBLK, HPAD), BF16),
            pltpu.VMEM((NQ, PBLK, HPAD), BF16),
            pltpu.VMEM((NQ, PBLK, HPAD), BF16),
            pltpu.VMEM((NQ, PBLK, HPAD), BF16),
            pltpu.VMEM((TOK, TOK), BF16),
            pltpu.VMEM((NJ, 8, 128), F32),
            pltpu.VMEM((NJ, 8, 128), F32),
            pltpu.VMEM((NE, 8, 128), F32),
            dma((6,)),
            dma((NQ, 3)), dma((NQ,)),
            dma((NQ, 6)), dma((NQ,)), dma((NQ,)), dma((NQ,)),
            dma((NQ, 5)), dma((NQ,)),
            dma((NQ, CUTS)), dma((NQ, CUTS)), dma((NQ, CUTS)), dma((NQ, CUTS)),
            dma((7,)), dma((7,)), dma((3,)), dma((3,)),
        ],
        compiler_params=pltpu.CompilerParams(
            collective_id=0, has_side_effects=True, vmem_limit_bytes=60 * 1024 * 1024
        ),
    )(upstream.T, expert_ids.T, router_logits.T, guard_mask.reshape(1, TOK), w_down, saved_hidden)
    gh, gd, gl = pl.pallas_call(
        hand_over,
        out_shape=outs,
        in_specs=[vmem] * 3,
        out_specs=(hbm, hbm, hbm),
        scratch_shapes=[dma((3,))],
        compiler_params=pltpu.CompilerParams(vmem_limit_bytes=8 * 1024 * 1024),
    )(*results)
    return gh, gd, gl.T


def solution(mesh):
    in_specs = (
        P(("dp", "ep"), None),
        P(("dp", "ep"), None),
        P(("dp", "ep"), None),
        P(("dp", "ep")),
        P("ep", None),
        P("ep", "dp"),
    )
    out_specs = (P("ep", "dp"), P("dp", "ep"), P(("dp", "ep"), None))
    return jax.shard_map(body, mesh=mesh, in_specs=in_specs, out_specs=out_specs, check_vma=False)
```

```python
import jax
import jax.numpy as jnp
from jax import lax
from jax.experimental import pallas as pl
from jax.experimental.pallas import tpu as pltpu
from jax.sharding import PartitionSpec as P

MESH = pl.DeviceIdType.MESH
F32 = jnp.float32
BF16 = jnp.bfloat16

NE = 4
NX = 4
NJ = 8
NZ = 16
CAP = 32
TOK = 128
D = 2880
BLK = 180
PBLK = 192
NQ = 8
QW = 2 * PBLK
HID = 360
HPAD = 384
COLS = 1024
CUTS = 4
PART = PBLK // CUTS
WLANE = BLK


def dot_nt(a, b):
    return lax.dot_general(a, b, (((1,), (1,)), ((), ())), preferred_element_type=F32)


def dot_nn(a, b):
    return lax.dot_general(a, b, (((1,), (0,)), ((), ())), preferred_element_type=F32)


def kernel(
    up_hbm, ids_hbm, logits_hbm, guard_hbm, w_hbm, h_hbm,
    gh, gd, gl,
    ids_ref, logits_ref, guard_ref, up, upf, upb, w, wblk, wq, h, scaled, cws, rows, g, acc,
    t_ref, sp, sm, rp, rm, sel, rs, rr, ri,
    in_sem, y_send, y_recv, x_send, xl_recv, xr_recv, xo_recv, s_send, s_recv,
    sp_send, rp_recv, sm_send, rm_recv, r1_send, r1_recv, r2_send, r2_recv,
):
    z = lax.axis_index("dp")
    ep = lax.axis_index("ep")
    y = ep // NJ
    j = ep % NJ
    x = j // 2
    c = j % 2
    zr = lax.rem(z + 1, NZ)
    zl = lax.rem(z + NZ - 1, NZ)
    jr = lax.rem(x + 1, NX) * 2 + c
    jl = lax.rem(x + NX - 1, NX) * 2 + c
    jo = lax.rem(x + 2, NX) * 2 + c
    js = x * 2 + (1 - c)

    cp_small = [
        pltpu.make_async_copy(ids_hbm, ids_ref, in_sem.at[3]),
        pltpu.make_async_copy(logits_hbm, logits_ref, in_sem.at[4]),
        pltpu.make_async_copy(guard_hbm, guard_ref, in_sem.at[5]),
    ]
    cp_up = pltpu.make_async_copy(up_hbm, up, in_sem.at[0])
    cp_h = pltpu.make_async_copy(h_hbm, h, in_sem.at[1])
    cp_w = pltpu.make_async_copy(w_hbm, w, in_sem.at[2])
    for cp in cp_small:
        cp.start()
    cp_up.start()
    cp_w.start()
    cp_h.start()

    barrier = pltpu.get_barrier_semaphore()
    for d in range(1, NJ):
        pl.semaphore_signal(barrier, 1, device_id=(z, y * NJ + lax.rem(j + d, NJ)), device_id_type=MESH)
    for d in range(1, NE):
        pl.semaphore_signal(barrier, 1, device_id=(z, lax.rem(y + d, NE) * NJ + j), device_id_type=MESH)
    pl.semaphore_signal(barrier, 1, device_id=(zr, ep), device_id_type=MESH)
    pl.semaphore_signal(barrier, 1, device_id=(zl, ep), device_id_type=MESH)

    for cp in cp_small:
        cp.wait()
    ids = ids_ref[...]
    logits = logits_ref[...]
    live = guard_ref[...] == 1
    top = jnp.max(logits, axis=0, keepdims=True)
    ex = jnp.exp(logits - top)
    probs = ex / jnp.sum(ex, axis=0, keepdims=True)
    combine = probs.astype(BF16).astype(F32)
    chosen = []
    weight = []
    for e in range(NE):
        hit = ((ids == e) & live).astype(F32)
        chosen.append(jnp.sum(hit, axis=0, keepdims=True))
        weight.append(jnp.sum(hit * combine, axis=0, keepdims=True))
    mask = jnp.concatenate(chosen + [jnp.zeros((8 - NE, TOK), F32)], axis=0)
    earlier = (
        lax.broadcasted_iota(jnp.int32, (TOK, TOK), 0) < lax.broadcasted_iota(jnp.int32, (TOK, TOK), 1)
    ).astype(F32).astype(BF16)
    slot = dot_nn(mask.astype(BF16), earlier)
    place = lax.broadcasted_iota(jnp.int32, (CAP, TOK), 0).astype(F32)
    picks = []
    wcols = []
    for e in range(NE):
        pick = jnp.where(slot[e:e + 1, :] == place, mask[e:e + 1, :], 0.0)
        picks.append(pick)
        wcols.append(jnp.sum(pick * weight[e], axis=1, keepdims=True))
    select = jnp.concatenate(picks, axis=0).astype(BF16)
    wcol = jnp.concatenate(wcols, axis=0)
    sel[...] = select
    at_weight = lax.broadcasted_iota(jnp.int32, (TOK, QW), 1) == WLANE

    cp_up.wait()
    upf[...] = up[...].astype(F32)
    gap = jnp.zeros((PBLK - BLK, TOK), F32)
    for b in range(NZ):
        upb[b] = jnp.concatenate([upf[b * BLK:(b + 1) * BLK, :], gap], axis=0).astype(BF16)

    def first(t):
        return lax.rem(z + 8 - t + NZ, NZ)

    def second(t):
        return lax.rem(z + 9 + t, NZ)

    def make_rows(t):
        part = jnp.concatenate([upb[first(t)], upb[second(t)]], axis=0)
        got = dot_nt(sel[...], part)
        rows[t] = jnp.where(at_weight, wcol, got).astype(BF16)
        g[t, 0, j] = rows[t, pl.ds(pl.multiple_of(y * CAP, CAP), CAP), :]

    def y_copy(t, d):
        e = lax.rem(y + d, NE)
        return pltpu.make_async_remote_copy(
            src_ref=rows.at[t, pl.ds(pl.multiple_of(e * CAP, CAP), CAP)],
            dst_ref=g.at[t, NE - d, j],
            send_sem=y_send.at[t, d - 1],
            recv_sem=y_recv.at[t],
            device_id=(z, e * NJ + j),
            device_id_type=MESH,
        )

    def x_copy(t, kind):
        ref, to, sem = [
            (g.at[t, 0, j], jr, xl_recv),
            (g.at[t, 0, j], jl, xr_recv),
            (g.at[t, pl.ds(1, 3), j], jr, xl_recv),
            (g.at[t, pl.ds(1, 3), j], jl, xr_recv),
            (g.at[t, pl.ds(0, 2), jl], jr, xo_recv),
            (g.at[t, pl.ds(2, 2), jr], jl, xo_recv),
        ][kind]
        return pltpu.make_async_remote_copy(
            src_ref=ref, dst_ref=ref, send_sem=x_send.at[t, kind], recv_sem=sem.at[t],
            device_id=(z, y * NJ + to), device_id_type=MESH,
        )

    def s_copy(t, kind):
        ref = [
            g.at[t, 0, j],
            g.at[t, pl.ds(1, 3), j],
            g.at[t, :, jl],
            g.at[t, :, jr],
            g.at[t, :, jo],
        ][kind]
        return pltpu.make_async_remote_copy(
            src_ref=ref, dst_ref=ref, send_sem=s_send.at[t, kind], recv_sem=s_recv.at[t],
            device_id=(z, y * NJ + js), device_id_type=MESH,
        )

    def wait_bytes(ref, sem):
        pltpu.make_async_copy(ref, ref, sem).wait()

    def start(t):
        for d in (2, 1, 3):
            y_copy(t, d).start()
        x_copy(t, 0).start()
        x_copy(t, 1).start()
        s_copy(t, 0).start()

    def rest(t):
        wait_bytes(g.at[t, pl.ds(1, 3), j], y_recv.at[t])
        x_copy(t, 2).start()
        x_copy(t, 3).start()
        s_copy(t, 1).start()

    def forward(t):
        wait_bytes(g.at[t, :, jl], xl_recv.at[t])
        x_copy(t, 4).start()
        s_copy(t, 2).start()
        wait_bytes(g.at[t, :, jr], xr_recv.at[t])
        x_copy(t, 5).start()
        s_copy(t, 3).start()

    def opposite(t):
        wait_bytes(g.at[t, :, jo], xo_recv.at[t])
        s_copy(t, 4).start()

    make_rows(0)
    pl.semaphore_wait(barrier, NJ - 1 + NE - 1 + 2)
    start(0)
    make_rows(1)
    start(1)
    make_rows(2)
    start(2)

    cp_w.wait()
    wgap = jnp.zeros((HID, PBLK - BLK), BF16)
    for b in range(NZ):
        wblk[b] = jnp.concatenate([w[:, b * BLK:(b + 1) * BLK], wgap], axis=1)

    def pair_w(t):
        wq[t] = jnp.concatenate([wblk[first(t)], wblk[second(t)]], axis=1)

    pair_w(0)
    rest(0)
    make_rows(3)
    start(3)
    rest(1)
    acc[...] = jnp.zeros_like(acc)
    pair_w(1)
    forward(0)
    make_rows(4)
    start(4)
    rest(2)
    cp_h.wait()
    forward(1)
    make_rows(5)
    start(5)
    rest(3)

    def plus_send(t, k):
        at = pl.ds(k * PART, PART)
        return pltpu.make_async_remote_copy(
            src_ref=sp.at[t, at], dst_ref=rp.at[t, at], send_sem=sp_send.at[t, k], recv_sem=rp_recv.at[t, k],
            device_id=(zr, ep), device_id_type=MESH,
        )

    def minus_send(t, k):
        at = pl.ds(k * PART, PART)
        return pltpu.make_async_remote_copy(
            src_ref=sm.at[t, at], dst_ref=rm.at[t, at], send_sem=sm_send.at[t, k], recv_sem=rm_recv.at[t, k],
            device_id=(zl, ep), device_id_type=MESH,
        )

    def chains(t, k):
        at = slice(k * PART, (k + 1) * PART)
        at2 = slice(PBLK + k * PART, PBLK + (k + 1) * PART)

        @pl.when(t == 0)
        def _():
            sp[t, at, :] = t_ref[at, :].astype(BF16)
            plus_send(t, k).start()
            sm[t, at, :] = t_ref[at2, :].astype(BF16)
            minus_send(t, k).start()

        @pl.when(t > 0)
        def _():
            wait_bytes(rp.at[t - 1, pl.ds(k * PART, PART)], rp_recv.at[t - 1, k])
            sp[t, at, :] = (t_ref[at, :] + rp[t - 1, at, :].astype(F32)).astype(BF16)
            plus_send(t, k).start()

        @pl.when((t > 0) & (t < NQ - 1))
        def _():
            wait_bytes(rm.at[t - 1, pl.ds(k * PART, PART)], rm_recv.at[t - 1, k])
            sm[t, at, :] = (t_ref[at2, :] + rm[t - 1, at, :].astype(F32)).astype(BF16)
            minus_send(t, k).start()

    def source(n):
        return lax.rem(n - y + NE, NE)

    def scale_columns():
        one = (lax.broadcasted_iota(jnp.int32, (8, 128), 1) == WLANE - 128).astype(F32).astype(BF16)
        for n in range(NE):
            dy = source(n)
            cols = slice(n * 256, (n + 1) * 256)
            cw = dot_nt(one, g[0, dy, :, :, 128:256].reshape(256, 128))
            cws[:, cols] = cw
            scaled[dy, 0:HID, :] = (cw[0:1, :] * h[:, cols].astype(F32)).astype(BF16)
            scaled[dy, HID:HPAD, :] = jnp.zeros((HPAD - HID, 256), BF16)

    def r1(d):
        to = lax.rem(j + d, NJ)
        return pltpu.make_async_remote_copy(
            src_ref=rs.at[to], dst_ref=rr.at[j], send_sem=r1_send.at[d - 1], recv_sem=r1_recv.at[d - 1],
            device_id=(z, y * NJ + to), device_id_type=MESH,
        )

    def inner_products():
        lane = lax.broadcasted_iota(jnp.int32, (1, 128), 1) // CAP
        sums = []
        for n in range(2 * NE):
            cols = slice(n * 128, (n + 1) * 128)
            sums.append(jnp.sum(h[:, cols].astype(F32) * acc[:, cols], axis=0, keepdims=True))
        table = jnp.concatenate(sums, axis=0)
        turned = [table] + [pltpu.roll(table, CAP * d, 1) for d in range(1, 4)]
        for i in range(NJ):
            line = jnp.zeros((1, 128), F32)
            for n in range(NE):
                src = turned[(n - i) % 4][2 * n + i // 4:2 * n + i // 4 + 1, :]
                line = jnp.where(lane == n, src, line)
            rs[i] = jnp.broadcast_to(line, (8, 128))
        for d in range(1, NJ):
            r1(d).start()
        rr[j] = rs[j]

    @pl.loop(0, NQ)
    def _(t):
        opposite(t)

        @pl.when(t + 6 < NQ)
        def _():
            make_rows(t + 6)
            start(t + 6)

        @pl.when(t + 4 < NQ)
        def _():
            rest(t + 4)

        @pl.when(t > 0)
        def _():
            chains(t - 1, 1)

        @pl.when(t + 2 < NQ)
        def _():
            pair_w(t + 2)
            forward(t + 2)

        @pl.when(t > 0)
        def _():
            chains(t - 1, 2)

        wait_bytes(g.at[t, :, pl.ds(0, 4)], s_recv.at[t])

        @pl.when(t == 0)
        def _():
            scale_columns()

        for n in range(NE):
            acc[:, n * 256:(n + 1) * 256] += dot_nt(wq[t], g[t, source(n)].reshape(256, QW))

        @pl.when(t == NQ - 1)
        def _():
            inner_products()

        @pl.when(t > 0)
        def _():
            chains(t - 1, 3)

        part = dot_nn(scaled[0], g[t, 0].reshape(256, QW))
        for dy in range(1, NE):
            part = part + dot_nn(scaled[dy], g[t, dy].reshape(256, QW))
        t_ref[...] = part.T
        chains(t, 0)

    for k in range(1, CUTS):
        chains(NQ - 1, k)

    gh[...] = (cws[0:1, :] * acc[...]).astype(BF16)

    for d in range(1, NJ):
        r1(d).wait_recv()
    total = rr[0]
    for i in range(1, NJ):
        total = total + rr[i]
    ri[y] = total

    def r2(d):
        to = lax.rem(y + d, NE)
        return pltpu.make_async_remote_copy(
            src_ref=ri.at[y], dst_ref=ri.at[y], send_sem=r2_send.at[d - 1], recv_sem=r2_recv.at[d - 1],
            device_id=(z, to * NJ + j), device_id_type=MESH,
        )

    for d in range(1, NE):
        r2(d).start()

    @pl.loop(0, NQ)
    def _(t):
        for d in range(1, NE):
            y_copy(t, d).wait_send()
        for kind in range(6):
            x_copy(t, kind).wait_send()
        for kind in range(5):
            s_copy(t, kind).wait_send()

    for k in range(CUTS):
        wait_bytes(rm.at[NQ - 2, pl.ds(k * PART, PART)], rm_recv.at[NQ - 2, k])
    t_ref[0:PBLK, :] = t_ref[PBLK:QW, :] + rm[NQ - 2].astype(F32)

    for d in range(1, NE):
        r2(d).wait_recv()
    lanes = lax.broadcasted_iota(jnp.int32, (8, 128), 1) // CAP
    subl = lax.broadcasted_iota(jnp.int32, (8, 128), 0)
    inner = jnp.zeros((8, 128), F32)
    for e in range(NE):
        moved = pltpu.roll(ri[e], lax.rem(CAP * (e + NE - y), 128), 1)
        inner = jnp.where((lanes == e) & (subl == e), moved, inner)
    hi = inner.astype(BF16)
    rem = inner - hi.astype(F32)
    mid = rem.astype(BF16)
    low = (rem - mid.astype(F32)).astype(BF16)
    selected = sel[...]
    found = dot_nn(hi, selected) + dot_nn(mid, selected) + dot_nn(low, selected)
    dprob = jnp.zeros((4, TOK), F32)
    for e in range(NE):
        dprob = dprob + jnp.where((ids == e) & live, found[e:e + 1, :], 0.0)
    gl[...] = probs * (dprob - jnp.sum(probs * dprob, axis=0, keepdims=True))

    for k in range(CUTS):
        wait_bytes(rp.at[NQ - 1, pl.ds(k * PART, PART)], rp_recv.at[NQ - 1, k])
    final = t_ref[0:PBLK, :] + rp[NQ - 1].astype(F32)
    gd[...] = final[0:BLK, 0:HID].astype(BF16)

    @pl.loop(0, NQ - 1)
    def _(t):
        for k in range(CUTS):
            plus_send(t, k).wait_send()
            minus_send(t, k).wait_send()

    for k in range(CUTS):
        plus_send(NQ - 1, k).wait_send()
    for d in range(1, NJ):
        r1(d).wait_send()
    for d in range(1, NE):
        r2(d).wait_send()


def hand_over(gh_in, gd_in, gl_in, gh_out, gd_out, gl_out, sem):
    copies = [
        pltpu.make_async_copy(a, b, sem.at[i])
        for i, (a, b) in enumerate([(gh_in, gh_out), (gd_in, gd_out), (gl_in, gl_out)])
    ]
    for cp in copies:
        cp.start()
    for cp in copies:
        cp.wait()


def body(upstream, router_logits, expert_ids, guard_mask, w_down, saved_hidden):
    dma = pltpu.SemaphoreType.DMA
    vmem = pl.BlockSpec(memory_space=pltpu.VMEM)
    hbm = pl.BlockSpec(memory_space=pltpu.HBM)
    outs = (
        jax.ShapeDtypeStruct((HID, COLS), BF16),
        jax.ShapeDtypeStruct((BLK, HID), BF16),
        jax.ShapeDtypeStruct((4, TOK), F32),
    )
    results = pl.pallas_call(
        kernel,
        out_shape=(pltpu.VMEM((HID, COLS), BF16), pltpu.VMEM((BLK, HID), BF16), pltpu.VMEM((4, TOK), F32)),
        in_specs=[hbm] * 6,
        out_specs=(vmem, vmem, vmem),
        scratch_shapes=[
            pltpu.VMEM((4, TOK), jnp.int32),
            pltpu.VMEM((4, TOK), F32),
            pltpu.VMEM((1, TOK), jnp.int32),
            pltpu.VMEM((D, TOK), BF16),
            pltpu.VMEM((D, TOK), F32),
            pltpu.VMEM((NZ, PBLK, TOK), BF16),
            pltpu.VMEM((HID, D), BF16),
            pltpu.VMEM((NZ, HID, PBLK), BF16),
            pltpu.VMEM((NQ, HID, QW), BF16),
            pltpu.VMEM((HID, COLS), BF16),
            pltpu.VMEM((NE, HPAD, 256), BF16),
            pltpu.VMEM((8, COLS), F32),
            pltpu.VMEM((NQ, TOK, QW), BF16),
            pltpu.VMEM((NQ, NE, NJ, CAP, QW), BF16),
            pltpu.VMEM((HID, COLS), F32),
            pltpu.VMEM((QW, HPAD), F32),
            pltpu.VMEM((NQ, PBLK, HPAD), BF16),
            pltpu.VMEM((NQ, PBLK, HPAD), BF16),
            pltpu.VMEM((NQ, PBLK, HPAD), BF16),
            pltpu.VMEM((NQ, PBLK, HPAD), BF16),
            pltpu.VMEM((TOK, TOK), BF16),
            pltpu.VMEM((NJ, 8, 128), F32),
            pltpu.VMEM((NJ, 8, 128), F32),
            pltpu.VMEM((NE, 8, 128), F32),
            dma((6,)),
            dma((NQ, 3)), dma((NQ,)),
            dma((NQ, 6)), dma((NQ,)), dma((NQ,)), dma((NQ,)),
            dma((NQ, 5)), dma((NQ,)),
            dma((NQ, CUTS)), dma((NQ, CUTS)), dma((NQ, CUTS)), dma((NQ, CUTS)),
            dma((7,)), dma((7,)), dma((3,)), dma((3,)),
        ],
        compiler_params=pltpu.CompilerParams(
            collective_id=0, has_side_effects=True, vmem_limit_bytes=60 * 1024 * 1024
        ),
    )(upstream.T, expert_ids.T, router_logits.T, guard_mask.reshape(1, TOK), w_down, saved_hidden)
    gh, gd, gl = pl.pallas_call(
        hand_over,
        out_shape=outs,
        in_specs=[vmem] * 3,
        out_specs=(hbm, hbm, hbm),
        scratch_shapes=[dma((3,))],
        compiler_params=pltpu.CompilerParams(vmem_limit_bytes=8 * 1024 * 1024),
    )(*results)
    return gh, gd, gl.T


def solution(mesh):
    in_specs = (
        P(("dp", "ep"), None),
        P(("dp", "ep"), None),
        P(("dp", "ep"), None),
        P(("dp", "ep")),
        P("ep", None),
        P("ep", "dp"),
    )
    out_specs = (P("ep", "dp"), P("dp", "ep"), P(("dp", "ep"), None))
    return jax.shard_map(body, mesh=mesh, in_specs=in_specs, out_specs=out_specs, check_vma=False)
```
